32 devices in a mesh: group: 2 (over x), rx: 16 (over z, y, core).
Axes of the slice: x: 2, y: 2, z: 4, core: 2. Of those that a mesh axis runs over, the one named last changes fastest.
Arguments:
- traces: bfloat16 [1024, 2, 512], P('rx', 'group'), parts along dimension 1, may hold values from -6 to 6
- cotangent: bfloat16 [1024, 2, 512], P('rx', 'group'), parts along dimension 1, may hold values from -6 to 6
- mute_mask: int32 [1024, 2], P('rx', 'group'), parts along dimension 1, may hold values 0 or 1
- dead_flags: int32 [1024], P('rx'), may hold values 0 or 1
- first_conv_weights: float32 [3, 64], replicated, may hold values from -3.5 to 3.5
- first_bias: float32 [64], replicated, may hold values from -3 to 3
- conv_taps: bfloat16 [3, 64, 64], replicated, may hold values from -0.4375 to 0.4375
- in_proj: bfloat16 [64, 64], replicated, may hold values from -0.1875 to 0.1875
- out_proj: bfloat16 [64, 64], replicated, may hold values from -0.1875 to 0.1875
- decay_rates: float32 [64], replicated, may hold values from 0 to 0.12
- low_rank: float32 [64], replicated, may hold values from -4 to 4
- mix_weights: float32 [64], replicated, may hold values from -0.75 to 0.75
- back_weights: float32 [64], replicated, may hold values from -4 to 4
- read_weights: float32 [64], replicated, may hold values from -0.75 to 0.75
- down_basis: bfloat16 [256, 1024], P(None, 'rx'), may hold values from -0.125 to 0.125
- up_basis: bfloat16 [1024, 256], P('rx'), may hold values from -0.5 to 0.5
Outputs:
- predicted: float32 [1024, 2, 512], P('rx', 'group'), parts along dimension 1
- grad_conv: float32 [6, 64, 64], P('group'), parts along dimension 0
- grad_in: float32 [128, 64], P('group'), parts along dimension 0
- grad_out: float32 [128, 64], P('group'), parts along dimension 0
- grad_down: float32 [512, 1024], P('group', 'rx'), parts along dimension 0
- grad_up: float32 [1024, 512], P('rx', 'group'), parts along dimension 1
The draws below stay inside these ranges and needn't reach their ends.
There are 2 independent parts, one for each index of `group`. The reference program is written for one: setup_inputs(seed, part) draws one part's arguments, and reference() takes and returns one part's arrays. A program takes and returns all parts, laid end to end along the dimension named above; an argument that names none is the same for every part. Nothing has to cross between parts.
All inputs are finite; a program needn't handle non-finite values. No bound on the sum of `mute_mask` or of `dead_flags` on one device may be relied on, other than what follows from the above.
Results may differ from the reference program's by a relative error of at most 0.02.
Values may be sent and summed in bfloat16 or wider, within the bound.
A program may use at most 128 MiB of HBM per device.

```python
import math
import jax
import jax.numpy as jnp
from jax import lax

SHOTS = 1
TW = 512
C = 64
N = 64
K = 256
KT = 3
FIRST_DILATION = 1
SECOND_DILATION = 4
NR = 1024


def draw_decay_rates(key, part):
    pick_key, slow_key, fast_key = jax.random.split(jax.random.fold_in(key, 11), 3)
    forgetful = jax.random.randint(pick_key, (N,), 0, 2) == 0
    slow_rate = jnp.exp(jax.random.uniform(slow_key, (N,), jnp.float32, math.log(0.2), math.log(1.2))) / NR
    fast_rate = jnp.exp(jax.random.uniform(fast_key, (N,), jnp.float32, math.log(0.06), math.log(0.12)))
    return jnp.where(forgetful, fast_rate, slow_rate).astype(jnp.float32)


def set_ends(result, own_key, least, largest):
    place = [jax.random.randint(jax.random.fold_in(own_key, axis), (), 0, length) for axis, length in enumerate(result.shape)]
    widest = result.shape.index(max(result.shape))
    beside = place[:widest] + [(place[widest] + 1) % result.shape[widest]] + place[widest + 1:]
    return result.at[tuple(place)].set(least).at[tuple(beside)].set(largest)


def raised(result, own_key, source, target, blocks, factor):
    owner, partner = [(jnp.arange(result.shape[dim]) // (result.shape[dim] // blocks)).reshape([-1 if axis == dim else 1 for axis in range(result.ndim)]) for dim in (source, target)]
    chosen = jax.random.permutation(own_key, blocks)[partner]
    strong = (owner == chosen) | (owner == (partner + blocks // 2) % blocks)
    return jnp.where(strong, factor * result, result)


def steps_of(key, shape, shards, low, top_value):
    gain, own = 1.0, jax.random.fold_in(key, 6)
    for dim, blocks in shards:
        draws = jnp.exp(jax.random.uniform(jax.random.fold_in(own, dim), (blocks,), jnp.float32, low / len(shards), top_value / len(shards)))
        gain = gain * jnp.repeat(draws, shape[dim] // blocks).reshape([-1 if axis == dim else 1 for axis in range(len(shape))])
    return gain


def bell_draw(key, shape, width, reach, cuts=(), held_as=jnp.bfloat16):
    loudness = steps_of(key, shape, cuts, -0.22, 0.18) if cuts else 1.0
    drawn = jax.random.normal(key, shape, jnp.float32) * width * loudness
    return jnp.minimum(jnp.maximum(drawn, -reach), reach).astype(held_as)


def noise_with(rng, shape, deviation, bound, pieces, heavy, held_as=jnp.bfloat16):
    drawn = deviation * jax.random.normal(rng, shape, jnp.float32)
    if pieces:
        drawn = drawn * steps_of(rng, shape, pieces, -0.22, 0.18)
    return jnp.clip(raised(drawn, jax.random.fold_in(rng, 3), *heavy), -bound, bound).astype(held_as)


def setup_inputs(seed: int = 0, part: int = 0) -> dict:
    keys = jax.random.split(jax.random.key(seed), 17)
    own_keys = jax.random.split(jax.random.fold_in(keys[16], part), 17)
    traces = bell_draw(own_keys[0], (NR, SHOTS, TW), 1.0, 6.0, ((0, 16),))
    cotangent = bell_draw(own_keys[1], (NR, SHOTS, TW), 1.0, 6.0, ((0, 16),))
    mute_mask = set_ends((jax.random.randint(own_keys[2], (NR, SHOTS), 0, NR) < 3).astype(jnp.int32), jax.random.fold_in(own_keys[2], 1), 0, 1)
    dead_flags = set_ends((jax.random.randint(keys[3], (NR,), 0, 16) < 1).astype(jnp.int32), jax.random.fold_in(keys[3], 1), 0, 1)
    first_conv_weights = bell_draw(keys[4], (KT, C), KT ** -0.5, 3.5, (), jnp.float32)
    first_bias = bell_draw(keys[5], (C,), 0.5, 3.0, (), jnp.float32)
    conv_taps = bell_draw(keys[6], (KT, C, C), (KT * C) ** -0.5, 0.4375)
    in_proj = bell_draw(keys[7], (N, C), (16 * C) ** -0.5, 0.1875)
    out_proj = bell_draw(keys[8], (C, N), (16 * N) ** -0.5, 0.1875)
    decay_rates = draw_decay_rates(jax.random.fold_in(keys[16], 71), part)
    low_rank = bell_draw(keys[10], (N,), 1.0, 4.0, (), jnp.float32)
    mix_weights = bell_draw(keys[11], (C,), C ** -0.5, 0.75, (), jnp.float32)
    back_weights = bell_draw(keys[12], (C,), 1.0, 4.0, (), jnp.float32)
    read_weights = bell_draw(keys[13], (C,), C ** -0.5, 0.75, (), jnp.float32)
    down_basis = noise_with(keys[14], (K, NR), (4 * NR) ** -0.5, 0.125, ((1, 16),), (1, 0, 16, 2.0))
    up_basis = noise_with(keys[15], (NR, K), K ** -0.5, 0.5, ((0, 16),), (0, 1, 16, 2.0))
    return {"traces": traces, "cotangent": cotangent, "mute_mask": mute_mask, "dead_flags": dead_flags, "first_conv_weights": first_conv_weights, "first_bias": first_bias, "conv_taps": conv_taps, "in_proj": in_proj, "out_proj": out_proj, "decay_rates": decay_rates, "low_rank": low_rank, "mix_weights": mix_weights, "back_weights": back_weights, "read_weights": read_weights, "down_basis": down_basis, "up_basis": up_basis}


BETA = 0.5
HIGH = lax.Precision.HIGHEST

def time_delay_samples(values, offset):
    if offset == 0:
        return values
    length = values.shape[-1]
    filler = jnp.zeros(values.shape[:-1] + (abs(offset),), values.dtype)
    if offset > 0:
        return jnp.concatenate([values[..., offset:], filler], axis=-1)
    return jnp.concatenate([filler, values[..., :length + offset]], axis=-1)

def silu_slope(values):
    logistic = jax.nn.sigmoid(values)
    return logistic * (1.0 + values * (1.0 - logistic))

def apply_decay(current, gain_row, decay_rows, unit_vector):
    projected = jnp.einsum('n,snt->st', unit_vector, current, precision=HIGH)
    return gain_row[:, None, None] * (decay_rows[None, :, None] * current - BETA * unit_vector[None, :, None] * projected[:, None, :])

def reference(traces, cotangent, mute_mask, dead_flags, first_conv_weights, first_bias, conv_taps, in_proj, out_proj, decay_rates, low_rank, mix_weights, back_weights, read_weights, down_basis, up_basis):
    input_trace = traces.astype(jnp.float32) * (1.0 - dead_flags.astype(jnp.float32))[:, None, None]
    first_conv_output = jnp.zeros(input_trace.shape[:2] + (C, input_trace.shape[2]), jnp.float32) + first_bias[None, None, :, None]
    for filter_tap in range(KT):
        first_conv_output = first_conv_output + first_conv_weights[filter_tap][None, None, :, None] * time_delay_samples(input_trace, (filter_tap - 1) * FIRST_DILATION)[:, :, None, :]
    first_hidden_layer = jax.nn.silu(first_conv_output).astype(jnp.bfloat16)
    pre_two = jnp.zeros(first_hidden_layer.shape, jnp.float32)
    for filter_tap in range(KT):
        delayed_trace = time_delay_samples(first_hidden_layer, (filter_tap - 1) * SECOND_DILATION).astype(jnp.float32)
        pre_two = pre_two + jnp.einsum('dc,rsct->rsdt', conv_taps[filter_tap].astype(jnp.float32), delayed_trace, precision=HIGH)
    hidden_two = (first_hidden_layer.astype(jnp.float32) + jax.nn.silu(pre_two)).astype(jnp.bfloat16)
    raw_drive = jnp.einsum('nc,rsct->rsnt', in_proj.astype(jnp.float32), hidden_two.astype(jnp.float32), precision=HIGH)
    drive = raw_drive - lax.optimization_barrier(jnp.mean(raw_drive, axis=-1, keepdims=True))
    decay_rows = jnp.exp(-decay_rates)
    unit_vector = low_rank * lax.rsqrt(jnp.sum(low_rank * low_rank) + 1e-06)
    gains = 1.0 - 0.25 * mute_mask.astype(jnp.float32)

    def forward_step(current, inputs):
        drive_row, gain_row = inputs
        current = apply_decay(current, gain_row, decay_rows, unit_vector) + drive_row
        return (current, current)
    zeros_state = jnp.zeros((SHOTS, N, TW), jnp.float32)
    final_state, states = lax.scan(forward_step, zeros_state, (drive, gains))
    states_low = states.astype(jnp.bfloat16)
    mixed = hidden_two.astype(jnp.float32) + jnp.einsum('cn,rsnt->rsct', out_proj.astype(jnp.float32), states_low.astype(jnp.float32), precision=HIGH)
    summary = jnp.einsum('c,rsct->rst', mix_weights, mixed, precision=HIGH).astype(jnp.bfloat16)
    bottleneck = jnp.einsum('kr,rst->kst', down_basis.astype(jnp.float32), summary.astype(jnp.float32), precision=HIGH)
    active = jnp.tanh(bottleneck).astype(jnp.bfloat16)
    spread = jnp.einsum('rk,kst->rst', up_basis.astype(jnp.float32), active.astype(jnp.float32), precision=HIGH)
    coupling = jnp.sum(read_weights * back_weights)
    predicted = jnp.einsum('c,rsct->rst', read_weights, mixed, precision=HIGH) + coupling * spread
    spread_grad = (coupling * cotangent.astype(jnp.float32)).astype(jnp.bfloat16)
    active_grad = jnp.einsum('rk,rst->kst', up_basis.astype(jnp.float32), spread_grad.astype(jnp.float32), precision=HIGH)
    bottle_grad = (active_grad * (1.0 - jnp.square(active.astype(jnp.float32)))).astype(jnp.bfloat16)
    grad_up = jnp.einsum('rst,kst->rk', spread_grad.astype(jnp.float32), active.astype(jnp.float32), precision=HIGH)
    grad_down = jnp.einsum('kst,rst->kr', bottle_grad.astype(jnp.float32), summary.astype(jnp.float32), precision=HIGH)
    summary_grad = jnp.einsum('kr,kst->rst', down_basis.astype(jnp.float32), bottle_grad.astype(jnp.float32), precision=HIGH)
    mixed_grad = read_weights[None, None, :, None] * cotangent.astype(jnp.float32)[:, :, None, :] + mix_weights[None, None, :, None] * summary_grad[:, :, None, :]
    mixed_low = mixed_grad.astype(jnp.bfloat16)
    source = jnp.einsum('cn,rsct->rsnt', out_proj.astype(jnp.float32), mixed_low.astype(jnp.float32), precision=HIGH)

    def backward_step(incoming, inputs):
        source_row, gain_row = inputs
        adjoint = source_row + incoming
        return (apply_decay(adjoint, gain_row, decay_rows, unit_vector), adjoint)
    first_carry, adjoints = lax.scan(backward_step, zeros_state, (source, gains), reverse=True)
    adjoints_low = adjoints.astype(jnp.bfloat16)
    adjoint_wide = adjoints_low.astype(jnp.float32)
    adjoint_centred = adjoint_wide - lax.optimization_barrier(jnp.mean(adjoint_wide, axis=-1, keepdims=True))
    grad_out = jnp.einsum('rsct,rsnt->cn', mixed_low.astype(jnp.float32), states_low.astype(jnp.float32), precision=HIGH)
    grad_in = jnp.einsum('rsnt,rsct->nc', adjoint_centred, hidden_two.astype(jnp.float32), precision=HIGH)
    hidden_grad = mixed_grad + jnp.einsum('nc,rsnt->rsct', in_proj.astype(jnp.float32), adjoint_centred, precision=HIGH)
    pre_grad = (hidden_grad * silu_slope(pre_two)).astype(jnp.bfloat16)
    tap_grads = []
    for filter_tap in range(KT):
        delayed_trace = time_delay_samples(first_hidden_layer, (filter_tap - 1) * SECOND_DILATION).astype(jnp.float32)
        tap_grads.append(jnp.einsum('rsdt,rsct->dc', pre_grad.astype(jnp.float32), delayed_trace, precision=HIGH))
    grad_conv = jnp.stack(tap_grads, axis=0)
    return (predicted, grad_conv, grad_in, grad_out, grad_down, grad_up)
```

```python
import math

import jax
import jax.numpy as jnp
from jax import lax
from jax.sharding import PartitionSpec as P

BETA = 0.5
HIGH = lax.Precision.HIGHEST
LOG_MUTE = math.log(0.75)
BF = jnp.bfloat16
F32 = jnp.float32


def delay(values, offset):
    if offset == 0:
        return values
    length = values.shape[-1]
    filler = jnp.zeros(values.shape[:-1] + (abs(offset),), values.dtype)
    if offset > 0:
        return jnp.concatenate([values[..., offset:], filler], axis=-1)
    return jnp.concatenate([filler, values[..., : length + offset]], axis=-1)


def high(a, b):
    return jnp.dot(a, b, precision=HIGH)


def low(a, b, dims=((1,), (0,))):
    return lax.dot_general(
        a.astype(BF), b.astype(BF), (dims, ((), ())), preferred_element_type=F32
    )


def powers(first, matrix, count):
    width = first.shape[0]
    rows = first
    have = 1
    while have < count:
        rows = jnp.concatenate([rows, high(rows, matrix)], axis=0)
        matrix = high(matrix, matrix)
        have *= 2
    return rows[: count * width], matrix


def toeplitz(v):
    r, c = v.shape
    w = jnp.concatenate([v, jnp.zeros_like(v)], axis=0)
    flat = jnp.tile(w, (r, 1))[: r * (2 * r - 1)]
    return flat.reshape(r, 2 * r - 1, c)[:, :r]


def untoeplitz(x):
    r, _, c = x.shape
    wide = jnp.concatenate([x, jnp.zeros_like(x)], axis=1)
    flat = wide.reshape(r * 2 * r, c)
    flat = jnp.concatenate([flat, jnp.zeros((r, c), x.dtype)], axis=0)
    return flat.reshape(r, 2 * r + 1, c)[:, :r].sum(axis=0)


def per_device(
    traces, cotangent, mute_mask, dead_flags, first_conv_weights, first_bias, conv_taps,
    in_proj, out_proj, decay_rates, low_rank, mix_weights, back_weights, read_weights,
    down_basis, up_basis,
):
    devices, mine = lax.axis_size("rx"), lax.axis_index("rx")
    nr, _, nt = traces.shape
    taps, nc = first_conv_weights.shape
    nn = in_proj.shape[0]
    nk = down_basis.shape[0]
    cot = cotangent[:, 0].astype(F32)
    u = low_rank * lax.rsqrt(jnp.sum(low_rank * low_rank) + 1e-06)
    matrix = jnp.diag(jnp.exp(-decay_rates)) - BETA * jnp.outer(u, u)
    inp = in_proj.astype(F32)
    outp = out_proj.astype(F32)
    av = high(read_weights, outp)
    bv = high(mix_weights, outp)
    first = jnp.concatenate([inp.T, jnp.eye(nn, dtype=F32)], axis=0)
    rows, shard_power = powers(first, matrix, nr)
    rows = rows.reshape(nr, nc + nn, nn)
    ip, pw = rows[:, :nc], rows[:, nc:]
    nexts = high(pw.reshape(nr * nn, nn), matrix).reshape(nr, nn, nn)
    dev_rows, _ = powers(jnp.eye(nn, dtype=F32), shard_power, devices)
    dev_pw = dev_rows.reshape(devices, nn, nn)
    muted = mute_mask[:, 0].astype(F32)
    order = jnp.arange(nr)
    count = jnp.sum(jnp.where(order[None] <= order[:, None], muted[None], 0.0), axis=1)
    total = jnp.sum(muted)
    lead = jnp.exp(LOG_MUTE * count)
    ratio = jnp.where(
        order[None] >= order[:, None],
        jnp.exp(LOG_MUTE * jnp.maximum(count[None, :] - count[:, None], 0.0)), 0.0,
    )
    tail = jnp.exp(LOG_MUTE * (total - count))
    wa = high(nexts.reshape(nr * nn, nn), av).reshape(nr, nn) * lead[:, None]
    wb = high(nexts.reshape(nr * nn, nn), bv).reshape(nr, nn) * lead[:, None]
    ka = toeplitz(jnp.einsum("qcn,n->qc", ip, av, precision=HIGH)) * ratio[:, :, None]
    kb = toeplitz(jnp.einsum("qcn,n->qc", ip, bv, precision=HIGH)) * ratio[:, :, None]
    kend = ip[::-1].swapaxes(1, 2) * tail[:, None, None]
    kmat = jnp.concatenate([kb, ka, kend], axis=1).astype(BF)
    q_local = low(wa, cot, ((0,), (0,)))
    p_local = low(wb, down_basis, ((0,), (1,)))
    coupling = jnp.sum(read_weights * back_weights)
    spread_grad = (coupling * cot).astype(BF)
    early = jnp.concatenate([p_local, q_local], axis=1).astype(BF)
    early = lax.all_gather(early, "rx")
    totals = lax.all_gather(total, "rx")
    partial_grad = low(up_basis, spread_grad, ((0,), (0,)))
    places = jnp.arange(devices)
    upto = jnp.sum(jnp.where(places[None] <= places[:, None], totals[None], 0.0), axis=1)
    reached = jnp.sum(jnp.where(places <= mine, totals, 0.0))
    entered = jnp.sum(jnp.where(places < mine, totals, 0.0))
    before = upto - totals
    later_gain = jnp.where(
        places > mine, jnp.exp(LOG_MUTE * jnp.maximum(before - reached, 0.0)), 0.0
    )
    earlier_gain = jnp.where(
        places < mine, jnp.exp(LOG_MUTE * jnp.maximum(entered - upto, 0.0)), 0.0
    )
    doubled = jnp.concatenate([dev_pw, dev_pw], axis=0)
    later_pw = lax.dynamic_slice_in_dim(
        doubled, devices - 1 - mine, devices, axis=0
    )
    reverse = doubled[::-1]
    earlier_pw = lax.dynamic_slice_in_dim(
        reverse, 2 * devices - 1 - (devices + mine - 1), devices, axis=0
    )
    later_w = (later_pw * later_gain[:, None, None]).transpose(1, 0, 2).reshape(nn, -1)
    earlier_w = (earlier_pw * earlier_gain[:, None, None]).transpose(1, 0, 2).reshape(nn, -1)
    pq = low(later_w, early.reshape(devices * nn, -1))
    p_mine, q_mine = pq[:, :nk], pq[:, nk:]
    signal = traces[:, 0].astype(F32) * (1.0 - dead_flags.astype(F32))[:, None]
    pre_one = first_bias[None, :, None]
    for j in range(taps):
        pre_one = pre_one + first_conv_weights[j][None, :, None] * delay(signal, j - 1)[:, None]
    h1 = (0.5 * pre_one * (1.0 + jnp.tanh(0.5 * pre_one))).astype(BF)
    h1s = jnp.concatenate([delay(h1, (j - 1) * 4) for j in range(taps)], axis=1)
    wide_taps = conv_taps.transpose(1, 0, 2).reshape(nc, taps * nc)
    pre_two = jnp.einsum("dx,rxt->rdt", wide_taps, h1s, preferred_element_type=F32)
    h2 = (h1.astype(F32) + 0.5 * pre_two * (1.0 + jnp.tanh(0.5 * pre_two))).astype(BF)
    direct_mix = jnp.einsum("c,rct->rt", mix_weights.astype(BF), h2, preferred_element_type=F32)
    direct_read = jnp.einsum("c,rct->rt", read_weights, h2.astype(F32), precision=HIGH)
    z = low(
        kmat.transpose(1, 0, 2).reshape(-1, nr * nc), h2.reshape(nr * nc, nt)
    )
    z = z - jnp.mean(z, axis=-1, keepdims=True)
    s_local = z[:nr] + direct_mix
    pred_local = z[nr : 2 * nr] + direct_read
    end = z[2 * nr :]
    partial = low(down_basis, s_local) + low(p_mine, end, ((0,), (0,)))
    both = lax.psum_scatter(
        jnp.concatenate(
            [partial.reshape(devices, -1, nt), partial_grad.reshape(devices, -1, nt)], axis=1
        ).reshape(-1, nt).astype(BF),
        "rx", scatter_dimension=0, tiled=True,
    ).astype(F32)
    ends = lax.all_gather(end.astype(BF), "rx")
    share = nk // devices
    act = jnp.tanh(both[:share])
    bg = both[share:] * (1.0 - act * act)
    shared = lax.all_gather(jnp.stack([act, bg]).astype(BF), "rx")
    active = shared[:, 0].reshape(nk, nt)
    bottle_grad = shared[:, 1].reshape(nk, nt)
    entering = low(earlier_w, ends.reshape(devices * nn, nt))
    summary = s_local + low(wb, entering)
    predicted = pred_local + low(wa, entering) + coupling * low(up_basis, active)
    grad_up = low(spread_grad, active, ((1,), (1,)))
    grad_down = low(bottle_grad, summary, ((1,), (1,)))
    sg = low(down_basis, bottle_grad, ((0,), (0,)))
    arriving = q_mine + low(p_mine, bottle_grad)
    s = jnp.concatenate([sg, cot, arriving], axis=0)
    s = s.astype(BF)
    s_total = jnp.sum(s.astype(F32), axis=-1)
    h2_mean = jnp.mean(h2.astype(F32), axis=-1)
    back = jnp.einsum("qjc,jt->qct", kmat, s, preferred_element_type=F32)
    back = back - jnp.mean(back, axis=-1, keepdims=True)
    mixed_grad = (
        read_weights[None, :, None] * cot[:, None] + mix_weights[None, :, None] * sg[:, None]
    )
    sig = 0.5 * (1.0 + jnp.tanh(0.5 * pre_two))
    pre_grad = ((mixed_grad + back) * (sig * (1.0 + pre_two * (1.0 - sig)))).astype(BF)
    local_conv = jnp.einsum("rdt,rxt->dx", pre_grad, h1s, preferred_element_type=F32)
    local_conv = local_conv.reshape(nc, taps, nc).transpose(1, 0, 2)
    f = jnp.einsum("jt,qct->qjc", s, h2, preferred_element_type=F32)
    f = f - s_total[None, :, None] * h2_mean[:, None, :]
    f_sg = untoeplitz(f[:, :nr] * ratio[:, :, None])
    f_cot = untoeplitz(f[:, nr : 2 * nr] * ratio[:, :, None])
    f_end = f[:, 2 * nr :] * tail[:, None, None]
    ma = high(pw.reshape(nr * nn, nn), av).reshape(nr, nn)
    mb = high(pw.reshape(nr * nn, nn), bv).reshape(nr, nn)
    local_in = (
        low(ma, f_cot, ((0,), (0,)))
        + low(mb, f_sg, ((0,), (0,)))
        + jnp.einsum("qnm,qmc->nc", pw[::-1].astype(BF), f_end.astype(BF),
                     preferred_element_type=F32)
    )
    z_cot = low(cot, entering, ((1,), (1,))) * lead[:, None]
    z_sg = low(sg, entering, ((1,), (1,))) * lead[:, None]
    x = jnp.stack(
        [
            jnp.einsum("qcn,qc->n", ip, ff, precision=HIGH)
            + jnp.einsum("qnm,qm->n", nexts, zz, precision=HIGH)
            for ff, zz in ((f_cot, z_cot), (f_sg, z_sg))
        ]
    )
    grad_conv, grad_in, x = lax.psum((local_conv, local_in, x), "rx")
    grad_out = read_weights[:, None] * x[0][None] + mix_weights[:, None] * x[1][None]
    return (predicted[:, None], grad_conv, grad_in, grad_out, grad_down, grad_up)


def solution(mesh):
    return jax.shard_map(
        per_device,
        mesh=mesh,
        in_specs=(
            P("rx", "group", None), P("rx", "group", None), P("rx", "group"), P("rx"),
            P(), P(), P(), P(), P(), P(), P(), P(), P(), P(), P(None, "rx"), P("rx", None),
        ),
        out_specs=(
            P("rx", "group", None), P("group", None, None), P("group", None),
            P("group", None), P("group", "rx"), P("rx", "group"),
        ),
        check_vma=False,
    )
```

```python
import functools
import math

import jax
import jax.numpy as jnp
from jax import lax
from jax.experimental import pallas as pl
from jax.experimental.pallas import tpu as pltpu
from jax.sharding import PartitionSpec as P

BETA = 0.5
HIGH = lax.Precision.HIGHEST
LOG_MUTE = math.log(0.75)
BF = jnp.bfloat16
F32 = jnp.float32
MESH = pl.DeviceIdType.MESH


def delay(values, offset):
    if offset == 0:
        return values
    length = values.shape[-1]
    filler = jnp.zeros(values.shape[:-1] + (abs(offset),), values.dtype)
    if offset > 0:
        return jnp.concatenate([values[..., offset:], filler], axis=-1)
    return jnp.concatenate([filler, values[..., : length + offset]], axis=-1)


def high(a, b):
    return jnp.dot(a, b, precision=HIGH)


def low(a, b, dims=((1,), (0,))):
    return lax.dot_general(
        a.astype(BF), b.astype(BF), (dims, ((), ())), preferred_element_type=F32
    )


def powers(first, matrix, count):
    width = first.shape[0]
    rows = first
    have = 1
    while have < count:
        rows = jnp.concatenate([rows, high(rows, matrix)], axis=0)
        matrix = high(matrix, matrix)
        have *= 2
    return rows[: count * width], matrix


def gain_from(count_ref, q, order):
    passed = jnp.maximum(count_ref[...] - count_ref[q : q + 1, :], 0.0)
    return jnp.where(order >= q, jnp.exp(LOG_MUTE * passed), 0.0)


def spread_kernel(v_ref, count_ref, out_ref):
    v = v_ref[...]
    order = lax.broadcasted_iota(jnp.int32, v.shape, 0)
    for q in range(v.shape[0]):
        moved = pltpu.roll(v, q, 0) if q else v
        out_ref[q] = (moved * gain_from(count_ref, q, order)).astype(out_ref.dtype)


def gather_kernel(x_ref, count_ref, out_ref):
    nr = x_ref.shape[0]
    order = lax.broadcasted_iota(jnp.int32, x_ref.shape[1:], 0)
    total = jnp.zeros(x_ref.shape[1:], F32)
    for q in range(nr):
        part = x_ref[q] * gain_from(count_ref, q, order)
        total = total + (pltpu.roll(part, nr - q, 0) if q else part)
    out_ref[...] = total


def whole_call(kernel, out_shape, *operands):
    return pl.pallas_call(
        kernel,
        out_shape=out_shape,
        compiler_params=pltpu.CompilerParams(vmem_limit_bytes=40 << 20),
    )(*operands)


def meet(devices):
    me = lax.axis_index("rx")
    barrier = pltpu.get_barrier_semaphore()

    def greet(i, c):
        pl.semaphore_signal(
            barrier, inc=1, device_id={"rx": lax.rem(me + i, devices)}, device_id_type=MESH
        )
        return c

    lax.fori_loop(1, devices, greet, 0)
    pl.semaphore_wait(barrier, devices - 1)
    return me


def sends(devices, me, pick, sems):
    def copy(i):
        peer = lax.rem(me + i, devices)
        src, dst = pick(peer)
        return pltpu.make_async_remote_copy(
            src_ref=src, dst_ref=dst, send_sem=sems[0].at[i], recv_sem=sems[1].at[i],
            device_id={"rx": peer}, device_id_type=MESH,
        )

    def start(i, c):
        copy(i).start()
        return c

    def wait(i, c):
        copy(i).wait()
        return c

    return (
        lambda: lax.fori_loop(1, devices, start, 0),
        lambda: lax.fori_loop(1, devices, wait, 0),
    )


def total_of(landed, devices):
    return lax.fori_loop(
        1, devices, lambda d, acc: acc + landed[d].astype(F32), landed[0].astype(F32)
    )


def middle_kernel(devices, x_ref, y_ref, shared_ref, ends_ref, landed, s0, r0, s1, r1, s2, r2):
    me = meet(devices)
    start, wait = sends(devices, me, lambda p: (x_ref.at[p], landed.at[me]), (s0, r0))
    start()
    start_y, wait_y = sends(devices, me, lambda p: (y_ref, ends_ref.at[me]), (s1, r1))
    start_y()
    landed[me] = x_ref[me]
    wait()
    both = total_of(landed, devices)
    act = jnp.tanh(both[0])
    bg = both[1] * (1.0 - act * act)
    shared_ref[me] = jnp.stack([act, bg]).astype(BF)
    start, wait = sends(devices, me, lambda p: (shared_ref.at[me], shared_ref.at[me]), (s2, r2))
    start()
    ends_ref[me] = y_ref[...]
    wait_y()
    wait()


def sum_kernel(devices, x_ref, out_ref, landed, s0, r0, s1, r1):
    me = meet(devices)
    start, wait = sends(devices, me, lambda p: (x_ref.at[p], landed.at[me]), (s0, r0))
    start()
    landed[me] = x_ref[me]
    wait()
    out_ref[me] = total_of(landed, devices)
    start, wait = sends(devices, me, lambda p: (out_ref.at[me], out_ref.at[me]), (s1, r1))
    start()
    wait()


def remote_call(kernel, devices, ident, pairs, landed, out_shape, *operands):
    return pl.pallas_call(
        functools.partial(kernel, devices),
        out_shape=out_shape,
        in_specs=[pl.BlockSpec(memory_space=pltpu.VMEM)] * len(operands),
        out_specs=jax.tree.map(lambda _: pl.BlockSpec(memory_space=pltpu.VMEM), out_shape),
        scratch_shapes=[landed] + [pltpu.SemaphoreType.DMA((devices,))] * (2 * pairs),
        compiler_params=pltpu.CompilerParams(
            collective_id=ident, has_side_effects=True, vmem_limit_bytes=40 << 20
        ),
    )(*operands)


def per_device(
    traces, cotangent, mute_mask, dead_flags, first_conv_weights, first_bias, conv_taps,
    in_proj, out_proj, decay_rates, low_rank, mix_weights, back_weights, read_weights,
    down_basis, up_basis,
):
    devices, mine = lax.axis_size("rx"), lax.axis_index("rx")
    nr, _, nt = traces.shape
    taps, nc = first_conv_weights.shape
    nn = in_proj.shape[0]
    nk = down_basis.shape[0]
    cot = cotangent[:, 0].astype(F32)
    u = low_rank * lax.rsqrt(jnp.sum(low_rank * low_rank) + 1e-06)
    matrix = jnp.diag(jnp.exp(-decay_rates)) - BETA * jnp.outer(u, u)
    inp = in_proj.astype(F32)
    outp = out_proj.astype(F32)
    av = high(read_weights, outp)
    bv = high(mix_weights, outp)
    first = jnp.concatenate([inp.T, jnp.eye(nn, dtype=F32)], axis=0)
    rows, shard_power = powers(first, matrix, nr)
    rows = rows.reshape(nr, nc + nn, nn)
    ip, pw = rows[:, :nc], rows[:, nc:]
    nexts = high(pw.reshape(nr * nn, nn), matrix).reshape(nr, nn, nn)
    dev_rows, _ = powers(jnp.eye(nn, dtype=F32), shard_power, devices)
    dev_pw = dev_rows.reshape(devices, nn, nn)
    muted = mute_mask[:, 0].astype(F32)
    order = jnp.arange(nr)
    count = jnp.sum(jnp.where(order[None] <= order[:, None], muted[None], 0.0), axis=1)
    total = jnp.sum(muted)
    lead = jnp.exp(LOG_MUTE * count)
    tail = jnp.exp(LOG_MUTE * (total - count))
    wa = high(nexts.reshape(nr * nn, nn), av).reshape(nr, nn) * lead[:, None]
    wb = high(nexts.reshape(nr * nn, nn), bv).reshape(nr, nn) * lead[:, None]
    base = jnp.concatenate(
        [jnp.einsum("qcn,n->qc", ip, v, precision=HIGH) for v in (bv, av)], axis=1
    )
    count_wide = jnp.broadcast_to(count[:, None], base.shape)
    kba = whole_call(
        spread_kernel, jax.ShapeDtypeStruct((nr, nr, 2 * nc), BF), base, count_wide
    )
    kend = (ip[::-1].swapaxes(1, 2) * tail[:, None, None]).astype(BF)
    kmat = jnp.concatenate([kba[:, :, :nc], kba[:, :, nc:], kend], axis=1)
    q_local = low(wa, cot, ((0,), (0,)))
    p_local = low(wb, down_basis, ((0,), (1,)))
    coupling = jnp.sum(read_weights * back_weights)
    spread_grad = (coupling * cot).astype(BF)
    coarse = jnp.floor(total / 128.0)
    lanes = jnp.arange(128)[None]
    tally = jnp.where(lanes == 0, coarse, jnp.where(lanes == 1, total - 128.0 * coarse, 0.0))
    early = jnp.concatenate(
        [p_local, q_local, jnp.broadcast_to(tally, (nn, 128))], axis=1
    ).astype(BF)
    early = lax.all_gather(early, "rx")
    tallies = early[:, 0, nk + nt :].astype(F32)
    totals = 128.0 * tallies[:, 0] + tallies[:, 1]
    partial_grad = low(up_basis, spread_grad, ((0,), (0,)))
    places = jnp.arange(devices)
    upto = jnp.sum(jnp.where(places[None] <= places[:, None], totals[None], 0.0), axis=1)
    reached = jnp.sum(jnp.where(places <= mine, totals, 0.0))
    entered = jnp.sum(jnp.where(places < mine, totals, 0.0))
    before = upto - totals
    later_gain = jnp.where(
        places > mine, jnp.exp(LOG_MUTE * jnp.maximum(before - reached, 0.0)), 0.0
    )
    earlier_gain = jnp.where(
        places < mine, jnp.exp(LOG_MUTE * jnp.maximum(entered - upto, 0.0)), 0.0
    )
    doubled = jnp.concatenate([dev_pw, dev_pw], axis=0)
    later_pw = lax.dynamic_slice_in_dim(
        doubled, devices - 1 - mine, devices, axis=0
    )
    reverse = doubled[::-1]
    earlier_pw = lax.dynamic_slice_in_dim(
        reverse, 2 * devices - 1 - (devices + mine - 1), devices, axis=0
    )
    later_w = (later_pw * later_gain[:, None, None]).transpose(1, 0, 2).reshape(nn, -1)
    earlier_w = (earlier_pw * earlier_gain[:, None, None]).transpose(1, 0, 2).reshape(nn, -1)
    pq = low(later_w, early[:, :, : nk + nt].reshape(devices * nn, -1))
    p_mine, q_mine = pq[:, :nk], pq[:, nk:]
    signal = traces[:, 0].astype(F32) * (1.0 - dead_flags.astype(F32))[:, None]
    pre_one = first_bias[None, :, None]
    for j in range(taps):
        pre_one = pre_one + first_conv_weights[j][None, :, None] * delay(signal, j - 1)[:, None]
    h1 = (0.5 * pre_one * (1.0 + jnp.tanh(0.5 * pre_one))).astype(BF)
    h1s = jnp.concatenate([delay(h1, (j - 1) * 4) for j in range(taps)], axis=1)
    wide_taps = conv_taps.transpose(1, 0, 2).reshape(nc, taps * nc)
    pre_two = jnp.einsum("dx,rxt->rdt", wide_taps, h1s, preferred_element_type=F32)
    h2 = (h1.astype(F32) + 0.5 * pre_two * (1.0 + jnp.tanh(0.5 * pre_two))).astype(BF)
    direct_mix = jnp.einsum("c,rct->rt", mix_weights.astype(BF), h2, preferred_element_type=F32)
    direct_read = jnp.einsum("c,rct->rt", read_weights, h2.astype(F32), precision=HIGH)
    z = low(
        kmat.transpose(1, 0, 2).reshape(-1, nr * nc), h2.reshape(nr * nc, nt)
    )
    z = z - jnp.mean(z, axis=-1, keepdims=True)
    s_local = z[:nr] + direct_mix
    pred_local = z[nr : 2 * nr] + direct_read
    end = z[2 * nr :]
    partial = low(down_basis, s_local) + low(p_mine, end, ((0,), (0,)))
    pieces = jnp.stack(
        [partial.reshape(devices, -1, 128), partial_grad.reshape(devices, -1, 128)], axis=1
    ).astype(BF)
    shared, ends = remote_call(
        middle_kernel, devices, 0, 3, pltpu.VMEM(pieces.shape, BF),
        (
            jax.ShapeDtypeStruct(pieces.shape, BF),
            jax.ShapeDtypeStruct((devices, nn, nt), BF),
        ),
        pieces, end.astype(BF),
    )
    active = shared[:, 0].reshape(nk, nt)
    bottle_grad = shared[:, 1].reshape(nk, nt)
    entering = low(earlier_w, ends.reshape(devices * nn, nt))
    summary = s_local + low(wb, entering)
    predicted = pred_local + low(wa, entering) + coupling * low(up_basis, active)
    grad_up = low(spread_grad, active, ((1,), (1,)))
    grad_down = low(bottle_grad, summary, ((1,), (1,)))
    sg = low(down_basis, bottle_grad, ((0,), (0,)))
    arriving = q_mine + low(p_mine, bottle_grad)
    s = jnp.concatenate([sg, cot, arriving], axis=0)
    s = s.astype(BF)
    s_total = jnp.sum(s.astype(F32), axis=-1)
    h2_mean = jnp.mean(h2.astype(F32), axis=-1)
    back = jnp.einsum("qjc,jt->qct", kmat, s, preferred_element_type=F32)
    back = back - jnp.mean(back, axis=-1, keepdims=True)
    mixed_grad = (
        read_weights[None, :, None] * cot[:, None] + mix_weights[None, :, None] * sg[:, None]
    )
    sig = 0.5 * (1.0 + jnp.tanh(0.5 * pre_two))
    pre_grad = ((mixed_grad + back) * (sig * (1.0 + pre_two * (1.0 - sig)))).astype(BF)
    local_conv = jnp.einsum("rdt,rxt->dx", pre_grad, h1s, preferred_element_type=F32)
    local_conv = local_conv.reshape(nc, taps, nc).transpose(1, 0, 2)
    f = jnp.einsum("jt,qct->qjc", s, h2, preferred_element_type=F32)
    f = f - s_total[None, :, None] * h2_mean[:, None, :]
    f_both = whole_call(
        gather_kernel, jax.ShapeDtypeStruct((nr, 2 * nc), F32),
        jnp.concatenate([f[:, :nr], f[:, nr : 2 * nr]], axis=2), count_wide,
    )
    f_sg, f_cot = f_both[:, :nc], f_both[:, nc:]
    f_end = f[:, 2 * nr :] * tail[:, None, None]
    ma = high(pw.reshape(nr * nn, nn), av).reshape(nr, nn)
    mb = high(pw.reshape(nr * nn, nn), bv).reshape(nr, nn)
    local_in = (
        low(ma, f_cot, ((0,), (0,)))
        + low(mb, f_sg, ((0,), (0,)))
        + jnp.einsum("qnm,qmc->nc", pw[::-1].astype(BF), f_end.astype(BF),
                     preferred_element_type=F32)
    )
    z_cot = low(cot, entering, ((1,), (1,))) * lead[:, None]
    z_sg = low(sg, entering, ((1,), (1,))) * lead[:, None]
    x = jnp.stack(
        [
            jnp.einsum("qcn,qc->n", ip, ff, precision=HIGH)
            + jnp.einsum("qnm,qm->n", nexts, zz, precision=HIGH)
            for ff, zz in ((f_cot, z_cot), (f_sg, z_sg))
        ]
    )
    flat = jnp.concatenate([local_conv.reshape(-1), local_in.reshape(-1), x.reshape(-1)])
    unit = devices * 8 * 128
    flat = jnp.pad(flat, (0, -flat.shape[0] % unit)).reshape(devices, -1, 128)
    flat = remote_call(
        sum_kernel, devices, 1, 2, pltpu.VMEM(flat.shape, F32),
        jax.ShapeDtypeStruct(flat.shape, F32), flat,
    ).reshape(-1)
    n_conv, n_in = local_conv.size, local_in.size
    grad_conv = flat[:n_conv].reshape(local_conv.shape)
    grad_in = flat[n_conv : n_conv + n_in].reshape(local_in.shape)
    x = flat[n_conv + n_in : n_conv + n_in + x.size].reshape(x.shape)
    grad_out = read_weights[:, None] * x[0][None] + mix_weights[:, None] * x[1][None]
    return (predicted[:, None], grad_conv, grad_in, grad_out, grad_down, grad_up)


def solution(mesh):
    return jax.shard_map(
        per_device,
        mesh=mesh,
        in_specs=(
            P("rx", "group", None), P("rx", "group", None), P("rx", "group"), P("rx"),
            P(), P(), P(), P(), P(), P(), P(), P(), P(), P(), P(None, "rx"), P("rx", None),
        ),
        out_specs=(
            P("rx", "group", None), P("group", None, None), P("group", None),
            P("group", None), P("group", "rx"), P("rx", "group"),
        ),
        check_vma=False,
    )
```
